512 devices in a mesh: section: 4 (over x_lo, core), seq: 64 (over z, y), batch: 2 (over x_hi).
Axes of the slice: x: 4 (x_hi: 2, x_lo: 2; x = x_hi * 2 + x_lo), y: 8, z: 8, core: 2. Of those that a mesh axis runs over, the one named last changes fastest.
Arguments:
- states: bfloat16 [4, 640, 3072], P('section', ('batch', 'seq')), parts along dimension 1, may hold values from -6 to 6
- step_index: int32 [1], replicated, may hold values from 0 to 27
- plan: int32 [29], replicated, may hold values from 0 to 1000, as said below
- time_weight: bfloat16 [3072, 256], P('seq'), may hold values from -0.375 to 0.375
- mod_weight: bfloat16 [4, 9216, 3072], P('section', 'seq'), may hold values from -0.109375 to 0.109375
- up_weight: bfloat16 [4, 12288, 3072], P('section', 'seq'), may hold values from -0.109375 to 0.109375
- down_weight: bfloat16 [4, 12288, 3072], P('section', 'seq'), may hold values from -0.0546875 to 0.0546875
Outputs:
- next_states: bfloat16 [4, 640, 3072], P('section', ('batch', 'seq')), parts along dimension 1
The draws below stay inside these ranges and needn't reach their ends.
There are 2 independent parts, one for each index of `batch`. The reference program is written for one: setup_inputs(seed, part) draws one part's arguments, and reference() takes and returns one part's arrays. A program takes and returns all parts, laid end to end along the dimension named above; an argument that names none is the same for every part. Nothing has to cross between parts.
Inputs may be any that keep to these rules, and one draw needn't show every extreme that they name: `plan`: strictly decreasing, first entry 1000, last entry 0.
All inputs are finite; a program needn't handle non-finite values.
Results may differ from the reference program's by a relative error of at most 0.007.
Values may be sent and summed in bfloat16 or wider, within the bound.
A program may use at most 64 MiB of HBM per device.

```python
import math
import jax
import jax.numpy as jnp
from jax import lax

D = 3072
FF = 12288
FREQ = 256
STEPS = 28
TOKENS = 320
N_SECTION = 4


def draw_plan(key, part):
    key = jax.random.fold_in(key, 7)
    picked = jax.random.permutation(key, 999)[:STEPS - 1] + 1
    inner = -jnp.sort(-picked.astype(jnp.int32))
    top = jnp.full((1,), 1000, jnp.int32)
    bottom = jnp.zeros((1,), jnp.int32)
    return jnp.concatenate([top, inner.astype(jnp.int32), bottom]).astype(jnp.int32)


def steps_of(rng, dims, cuts, smallest, largest):
    level = 1.0
    for dim, shards_of in cuts:
        draws = jax.random.uniform(jax.random.fold_in(jax.random.fold_in(rng, 6), dim), (shards_of,), jnp.float32, smallest / len(cuts), largest / len(cuts))
        level = level * jnp.repeat(jnp.exp(draws), dims[dim] // shards_of).reshape((-1,) + (1,) * (len(dims) - 1 - dim))
    return level


def normal_values(rng, dims, scale, most, shards=(), kind=jnp.bfloat16):
    factor_of = steps_of(rng, dims, shards, -0.22, 0.18) if shards else 1.0
    result = jax.random.normal(rng, dims, jnp.float32) * scale * factor_of
    return jnp.minimum(jnp.maximum(result, -most), most).astype(kind)


def setup_inputs(seed: int = 0, part: int = 0) -> dict:
    streams_of = jax.random.split(jax.random.key(seed), 8)
    part_keys = jax.random.split(jax.random.fold_in(streams_of[7], part), 8)
    return {
        "states": normal_values(part_keys[0], (N_SECTION, TOKENS, D), 1.0, 6.0, ((0, 4), (1, 64))),
        "step_index": jax.random.randint(streams_of[1], (1,), 0, STEPS).astype(jnp.int32),
        "plan": draw_plan(jax.random.fold_in(streams_of[7], 71), part),
        "time_weight": normal_values(streams_of[3], (D, FREQ), FREQ ** -0.5, 0.375, ((0, 64),)),
        "mod_weight": normal_values(streams_of[4], (N_SECTION, 3 * D, D), D ** -0.5, 0.109375, ((0, 4), (1, 64))),
        "up_weight": normal_values(streams_of[5], (N_SECTION, FF, D), D ** -0.5, 0.109375, ((0, 4), (1, 64))),
        "down_weight": normal_values(streams_of[6], (N_SECTION, FF, D), FF ** -0.5, 0.0546875, ((0, 4), (1, 64))),
    }


def embed_time(step_index, plan):
    sigma = plan[step_index[0]].astype(jnp.float32) / 1000.0
    sigma_next = plan[step_index[0] + 1].astype(jnp.float32) / 1000.0
    half = FREQ // 2
    freqs = jnp.exp(-math.log(10000.0) * jnp.arange(half, dtype=jnp.float32) / half)
    angles = 1000.0 * sigma * freqs
    feature = jnp.concatenate([jnp.cos(angles), jnp.sin(angles)])[None, :].astype(jnp.bfloat16)
    return (sigma, sigma_next, feature)

def reference(states, step_index, plan, time_weight, mod_weight, up_weight, down_weight):
    sigma, sigma_next, feature = embed_time(step_index, plan)
    cond = jax.nn.silu(jnp.dot(feature, time_weight.T, preferred_element_type=jnp.float32)).astype(jnp.bfloat16)
    outputs = []
    for group in range(N_SECTION):
        modul = jnp.dot(cond, mod_weight[group].T, preferred_element_type=jnp.float32)
        shift, scale, gate = (modul[:, :D], modul[:, D:2 * D], modul[:, 2 * D:])
        rows = states[group].astype(jnp.float32)
        center = rows - lax.optimization_barrier(jnp.mean(rows, axis=-1, keepdims=True))
        spread = lax.optimization_barrier(jnp.mean(center * center, axis=-1, keepdims=True))
        normed = (center * jax.lax.rsqrt(spread + 1e-06) * (1.0 + scale) + shift).astype(jnp.bfloat16)
        hidden = jax.nn.gelu(jnp.dot(normed, up_weight[group].T, preferred_element_type=jnp.float32), approximate=True).astype(jnp.bfloat16)
        branch = jnp.dot(hidden, down_weight[group], preferred_element_type=jnp.float32)
        outputs.append((rows + gate * branch).astype(jnp.bfloat16))
    first = (states[0].astype(jnp.float32) + (sigma_next - sigma) * outputs[-1].astype(jnp.float32)).astype(jnp.bfloat16)
    return jnp.stack([first] + outputs[:-1])
```

```python
import functools
import math

import jax
import jax.numpy as jnp
from jax import lax
from jax.experimental import pallas as pl
from jax.experimental.pallas import tpu as pltpu
from jax.sharding import PartitionSpec as P

MESH = pl.DeviceIdType.MESH
F32 = jnp.float32
BF16 = jnp.bfloat16
N = 8
LANES = 128
TOK = 5
CHUNKS = 24
USED = TOK * CHUNKS
ROWS = 128
PER = 48
MOD = 144
OFFSETS = (0, 1, -1, 2, -2, 3, -3, 4)


def by_rows(left, right):
    return lax.dot_general(
        left, right, (((1,), (1,)), ((), ())), preferred_element_type=F32
    )


def kernel(
    states_ref, step_ref, plan_ref, time_ref, mod_hbm, up_hbm, down_hbm,
    out_ref,
    mod_w, up_w, down_w, scaled_w, time_pad, cond_stage, cond_y, cond_z, cond_rows,
    mod_stage, mod_sum, mod_y, mod_z, shift_rows, bias_ref,
    own_f32, own, gathered, unpack, tokens, partial, pack, rs_in, final_in, final_out,
    gate_pack, raw_pack, out_send, out_recv,
    w_sem, small_send, small_recv, g_send, g_recv, rs_send, rs_recv, f_send, f_recv, s_send, s_recv,
):
    section = lax.axis_index("section")
    seq = lax.axis_index("seq")
    z, y = seq // N, lax.rem(seq, N)
    odd = lax.rem(y + z, 2)

    def at(yy, zz):
        return zz * N + yy

    def plus(v, k):
        return lax.rem(v + k + N, N)

    ring_y = [at(plus(y, k), z) for k in range(1, N)]
    ring_z = [at(y, plus(z, k)) for k in range(1, N)]
    far_first = (3, 2, 4, 1, 5, 0, 6)

    barrier = pltpu.get_barrier_semaphore()
    for q in ring_y + ring_z:
        pl.semaphore_signal(barrier, inc=1, device_id={"seq": q}, device_id_type=MESH)
    next_section = lax.rem(section + 1, 4)
    prev_section = lax.rem(section + 3, 4)
    for q in (next_section, prev_section):
        pl.semaphore_signal(barrier, inc=1, device_id={"section": q}, device_id_type=MESH)

    loads = []
    for i, (src, dst) in enumerate(((mod_hbm, mod_w), (up_hbm, up_w), (down_hbm, down_w))):
        copy = pltpu.make_async_copy(src.at[0], dst, w_sem.at[i])
        copy.start()
        loads.append(copy)

    index = step_ref[0]
    sigma = plan_ref[index].astype(F32) / 1000.0
    sigma_next = plan_ref[index + 1].astype(F32) / 1000.0
    lane = lax.broadcasted_iota(jnp.int32, (16, LANES), 1).astype(F32)
    angles = (1000.0 * sigma) * jnp.exp(lane * (-math.log(10000.0)) / LANES)
    feature = jnp.concatenate([jnp.cos(angles), jnp.sin(angles)], axis=1).astype(BF16)
    time_pad[...] = jnp.zeros_like(time_pad)
    time_pad[pl.ds(pl.multiple_of(y * PER, 16), PER), :] = time_ref[...]
    cond = by_rows(feature, time_pad[...])
    cond = (cond * jax.nn.sigmoid(cond)).astype(BF16).astype(F32)
    cond_stage[...] = jnp.zeros_like(cond_stage)
    for m in range(3):
        cond_stage[0, m : m + 1, :] = cond[0:1, m * LANES : (m + 1) * LANES]
    cond_y[y] = cond_stage[0]

    rows = states_ref[0].astype(F32)
    center = rows - jnp.mean(rows, axis=-1, keepdims=True)
    spread = jnp.mean(center * center, axis=-1, keepdims=True)
    normed = center * lax.rsqrt(spread + 1e-06)
    own_f32[USED:ROWS, :] = jnp.zeros((ROWS - USED, LANES), F32)
    raw_pack[USED:ROWS, :] = jnp.zeros((ROWS - USED, LANES), F32)
    gate_pack[USED:ROWS, :] = jnp.zeros((ROWS - USED, LANES), F32)
    for c in range(CHUNKS):
        own_f32[TOK * c : TOK * c + TOK, :] = normed[:, c * LANES : (c + 1) * LANES]
        raw_pack[TOK * c : TOK * c + TOK, :] = rows[:, c * LANES : (c + 1) * LANES]
    own[...] = own_f32[...].astype(BF16)
    for i in range(8):
        pack[i, USED:ROWS, :] = jnp.zeros((ROWS - USED, LANES), F32)

    pl.semaphore_wait(barrier, 16)

    def send(src, dst, ssem, rsem, q):
        pltpu.make_async_remote_copy(
            src_ref=src, dst_ref=dst, send_sem=ssem, recv_sem=rsem,
            device_id={"seq": q}, device_id_type=MESH,
        ).start()

    def wait(ref, sem):
        pltpu.make_async_copy(ref, ref, sem).wait()

    for k in far_first:
        send(cond_stage.at[0], cond_y.at[y], small_send.at[0], small_recv.at[0], ring_y[k])

    local = pltpu.make_async_copy(own, gathered.at[seq], g_recv.at[seq])
    local.start()
    for k in far_first:
        send(own, gathered.at[seq], g_send.at[0], g_recv.at[seq], ring_y[k] + odd * (ring_z[k] - ring_y[k]))

    wait(cond_y.at[0:7], small_recv.at[0])
    total = cond_y[0]
    for i in range(1, N):
        total = total + cond_y[i]
    cond_stage[1] = total
    cond_z[z] = total
    for k in far_first:
        send(cond_stage.at[1], cond_z.at[z], small_send.at[1], small_recv.at[1], ring_z[k])

    up_z, down_z = at(y, plus(z, 1)), at(y, plus(z, -1))
    up_y, down_y = at(plus(y, 1), z), at(plus(y, -1), z)

    def source(odd_class, offset, j):
        if odd_class:
            yy = plus(y, offset)
            return at(yy, 2 * j + lax.rem(yy + 1, 2))
        zz = plus(z, offset)
        return at(2 * j + lax.rem(zz, 2), zz)

    def forward(src, q):
        send(gathered.at[src], gathered.at[src], g_send.at[0], g_recv.at[src], q)

    def slab(offset, odd_class):
        return OFFSETS.index(offset) * 2 + odd_class

    def unpack_slab(offset, odd_class):
        s = slab(offset, odd_class)
        for j in range(4):
            unpack[j] = gathered[source(odd_class, offset, j)].astype(F32)
        for pair in range(2):
            for c in range(CHUNKS):
                both = jnp.concatenate(
                    [
                        unpack[2 * pair, TOK * c : TOK * c + 8, :],
                        unpack[2 * pair + 1, TOK * c : TOK * c + 8, :],
                    ],
                    axis=0,
                )
                tokens[s, 16 * pair : 16 * pair + 16, c * LANES : (c + 1) * LANES] = both.astype(BF16)

    def arrive(offset, odd_class, j):
        src = source(odd_class, offset, j)
        wait(gathered.at[src], g_recv.at[src])
        return src

    for j in range(4):
        for odd_class in (0, 1):
            src = arrive(0, odd_class, j)
            up, down = (up_y, down_y) if odd_class else (up_z, down_z)
            forward(src, up)
            forward(src, down)

    unpack_slab(0, 0)
    unpack_slab(0, 1)

    wait(cond_z.at[0:7], small_recv.at[1])
    for zz in range(N):
        for m in range(3):
            q = zz * 3 + m
            cond_rows[:, q * LANES : (q + 1) * LANES] = jnp.broadcast_to(
                cond_z[zz, m : m + 1, :], (16, LANES)
            ).astype(BF16)
    loads[0].wait()
    modul = by_rows(cond_rows[...], mod_w[...])[0:8]
    wide = jnp.concatenate([modul, jnp.zeros((8, N * MOD - MOD), F32)], axis=1)
    placed = jnp.zeros((8, N * MOD), F32)
    for yy in range(N):
        moved = pltpu.roll(wide, yy * MOD, 1) if yy else wide
        placed = jnp.where(y == yy, moved, placed)
    mod_stage[...] = jnp.zeros_like(mod_stage)
    for m in range(9):
        mod_stage[m : m + 1, :] = placed[0:1, m * LANES : (m + 1) * LANES]
    mod_y[y] = mod_stage[...]
    for k in far_first:
        send(mod_stage, mod_y.at[y], small_send.at[2], small_recv.at[2], ring_y[k])

    def gather_step(h):
        for j in range(4):
            for odd_class in (0, 1):
                up, down = (up_y, down_y) if odd_class else (up_z, down_z)
                src = arrive(-h, odd_class, j)
                if h < 3 or j < 2:
                    forward(src, up)
                src = arrive(h, odd_class, j)
                if h < 3 or j >= 2:
                    forward(src, down)

    def unpack_step(h):
        for odd_class in (0, 1):
            unpack_slab(h, odd_class)
            unpack_slab(-h, odd_class)

    gather_step(1)
    unpack_step(1)
    gather_step(2)

    wait(mod_y.at[0:7], small_recv.at[2])
    total = mod_y[0]
    for i in range(1, N):
        total = total + mod_y[i]
    mod_sum[...] = total
    mod_z[z] = total
    for k in far_first:
        send(mod_sum, mod_z.at[z], small_send.at[3], small_recv.at[3], ring_z[k])

    unpack_step(2)
    gather_step(3)
    unpack_step(3)
    for j in range(4):
        for odd_class in (0, 1):
            arrive(4, odd_class, j)
    unpack_slab(4, 0)
    unpack_slab(4, 1)

    wait(mod_z.at[0:7], small_recv.at[3])

    def modulation(q):
        return mod_z[q // 9, q % 9 : q % 9 + 1, :]

    loads[1].wait()
    first = lax.broadcasted_iota(jnp.int32, (16, LANES), 0)
    for c in range(CHUNKS):
        lanes = slice(c * LANES, (c + 1) * LANES)
        scale = 1.0 + modulation(CHUNKS + c)
        scaled_w[:, lanes] = (up_w[:, lanes].astype(F32) * scale).astype(BF16)
        shift = modulation(c)
        high = shift.astype(BF16).astype(F32)
        low = shift - high
        shift_rows[:, lanes] = jnp.where(first == 0, high, jnp.where(first == 1, low, 0.0)).astype(BF16)
    both = by_rows(shift_rows[...], up_w[...])
    bias_ref[...] = jnp.broadcast_to(both[0:1] + both[1:2], bias_ref.shape)
    loads[2].wait()

    def compute(first_slab, count):
        m = count * 32
        left = tokens[first_slab : first_slab + count].reshape(m, CHUNKS * LANES)
        hidden = jax.nn.gelu(by_rows(left, scaled_w[...]) + bias_ref[0:1, :], approximate=True).astype(BF16)
        for half in range(0, count * 4, 8):
            part = hidden[half * 8 : half * 8 + 64]
            for c4 in range(0, CHUNKS, 4):
                term = jnp.dot(
                    part, down_w[:, c4 * LANES : (c4 + 4) * LANES], preferred_element_type=F32
                )
                for i in range(8):
                    for c in range(4):
                        r = TOK * (c4 + c)
                        pack[i, r : r + TOK, :] = term[8 * i : 8 * i + TOK, c * LANES : (c + 1) * LANES]
            for i in range(8):
                b = half + i
                partial[first_slab + b // 4, b % 4] = pack[i].astype(BF16)

    towards = (up_z, down_z, up_y, down_y)

    def rs_send_to(direction, step, j):
        k = 5 - step
        offset = k if direction % 2 == 0 or k == 4 else -k
        send(
            partial.at[slab(offset, direction // 2), j], rs_in.at[direction, step - 1, j],
            rs_send.at[0], rs_recv.at[direction, step - 1, j], towards[direction],
        )

    def rs_add(direction, step, j):
        k = 5 - step
        offset = k if direction % 2 == 0 else -k
        ref = rs_in.at[direction, step - 2, j]
        wait(ref, rs_recv.at[direction, step - 2, j])
        s = slab(offset, direction // 2)
        partial[s, j] = (partial[s, j].astype(F32) + ref[...].astype(F32)).astype(BF16)

    def halves(direction):
        return (0, 1) if direction % 2 == 0 else (2, 3)

    compute(14, 2)
    for i in range(2):
        for direction in range(4):
            rs_send_to(direction, 1, halves(direction)[i])
    compute(10, 4)
    for i in range(2):
        for direction in range(4):
            rs_send_to(direction, 2, halves(direction + 1)[i])
    for i in range(2):
        for direction in range(4):
            j = halves(direction)[i]
            rs_add(direction, 2, j)
            rs_send_to(direction, 2, j)
    compute(6, 4)
    for step in (3, 4):
        for j in (2, 3, 0, 1):
            for direction in range(4):
                jj = j if direction % 2 == 0 else 3 - j
                rs_add(direction, step, jj)
                rs_send_to(direction, step, jj)
        if step == 3:
            compute(2, 4)
    compute(0, 2)

    for c in range(CHUNKS):
        gate_pack[TOK * c : TOK * c + TOK, :] = jnp.broadcast_to(modulation(2 * CHUNKS + c), (TOK, LANES))

    for j in (2, 3, 0, 1):
        for odd_class in (0, 1):
            value = partial[slab(0, odd_class), j].astype(F32)
            for direction in (2 * odd_class, 2 * odd_class + 1):
                ref = rs_in.at[direction, 3, j]
                wait(ref, rs_recv.at[direction, 3, j])
                value = value + ref[...].astype(F32)
            final_out[odd_class, j] = value.astype(BF16)
            target = source(odd_class, 0, j)
            mine = z if odd_class else y

            @pl.when(target != seq)
            def _(odd_class=odd_class, j=j, target=target, mine=mine):
                send(final_out.at[odd_class, j], final_in.at[mine], f_send.at[0], f_recv.at[0], target)

            @pl.when(target == seq)
            def _(odd_class=odd_class, j=j, mine=mine):
                pltpu.make_async_copy(final_out.at[odd_class, j], final_in.at[mine], f_recv.at[0]).start()

    wait(final_in, f_recv.at[0])
    branch = final_in[0].astype(F32)
    for i in range(1, N):
        branch = branch + final_in[i].astype(F32)
    out_send[...] = (raw_pack[...] + gate_pack[...] * branch).astype(BF16)
    shift_copy = pltpu.make_async_remote_copy(
        src_ref=out_send, dst_ref=out_recv, send_sem=s_send.at[0], recv_sem=s_recv.at[0],
        device_id={"section": next_section}, device_id_type=MESH,
    )
    shift_copy.start()

    for i, ref in enumerate((cond_y, cond_z, mod_y, mod_z)):
        wait(ref.at[0:7], small_send.at[i])
    wait(gathered.at[0:63], g_send.at[0])
    wait(partial.at[0:14], rs_send.at[0])
    wait(final_in.at[0:7], f_send.at[0])
    shift_copy.wait()

    received = out_recv[...].astype(F32)
    moved = raw_pack[...] + (sigma_next - sigma) * received
    own_f32[...] = jnp.where(section == 0, moved, received)
    for c in range(CHUNKS):
        out_ref[0, :, c * LANES : (c + 1) * LANES] = own_f32[TOK * c : TOK * c + TOK, :].astype(BF16)


def local(states, step_index, plan, time_weight, mod_weight, up_weight, down_weight):
    vmem = pl.BlockSpec(memory_space=pltpu.VMEM)
    smem = pl.BlockSpec(memory_space=pltpu.SMEM)
    anywhere = pl.BlockSpec(memory_space=pl.ANY)
    dma = pltpu.SemaphoreType.DMA
    width = states.shape[2]
    hidden = up_weight.shape[1]
    block = (ROWS, LANES)
    return pl.pallas_call(
        kernel,
        out_shape=jax.ShapeDtypeStruct(states.shape, states.dtype),
        in_specs=[vmem, smem, smem, vmem, anywhere, anywhere, anywhere],
        out_specs=vmem,
        scratch_shapes=[
            pltpu.VMEM((MOD, width), BF16),
            pltpu.VMEM((hidden, width), BF16),
            pltpu.VMEM((hidden, width), BF16),
            pltpu.VMEM((hidden, width), BF16),
            pltpu.VMEM((N * PER, 256), BF16),
            pltpu.VMEM((2, 8, LANES), F32),
            pltpu.VMEM((N, 8, LANES), F32),
            pltpu.VMEM((N, 8, LANES), F32),
            pltpu.VMEM((16, width), BF16),
            pltpu.VMEM((16, LANES), F32),
            pltpu.VMEM((16, LANES), F32),
            pltpu.VMEM((N, 16, LANES), F32),
            pltpu.VMEM((N, 16, LANES), F32),
            pltpu.VMEM((16, width), BF16),
            pltpu.VMEM((8, hidden), F32),
            pltpu.VMEM(block, F32),
            pltpu.VMEM(block, BF16),
            pltpu.VMEM((64,) + block, BF16),
            pltpu.VMEM((4,) + block, F32),
            pltpu.VMEM((16, 32, width), BF16),
            pltpu.VMEM((16, 4) + block, BF16),
            pltpu.VMEM((8,) + block, F32),
            pltpu.VMEM((4, 4, 4) + block, BF16),
            pltpu.VMEM((N,) + block, BF16),
            pltpu.VMEM((2, 4) + block, BF16),
            pltpu.VMEM(block, F32),
            pltpu.VMEM(block, F32),
            pltpu.VMEM(block, BF16),
            pltpu.VMEM(block, BF16),
            dma((3,)), dma((4,)), dma((4,)), dma((1,)), dma((64,)),
            dma((1,)), dma((4, 4, 4)), dma((1,)), dma((1,)), dma((1,)), dma((1,)),
        ],
        name="denoise",
        cost_estimate=pl.CostEstimate(flops=800_000_000, bytes_accessed=3_300_000, transcendentals=100_000),
        compiler_params=pltpu.CompilerParams(
            collective_id=0, has_side_effects=True, vmem_limit_bytes=40 * 1024 * 1024
        ),
    )(states, step_index, plan, time_weight, mod_weight, up_weight, down_weight)


def solution(mesh):
    in_specs = (
        P("section", ("batch", "seq"), None),
        P(),
        P(),
        P("seq", None),
        P("section", "seq", None),
        P("section", "seq", None),
        P("section", "seq", None),
    )
    out_specs = P("section", ("batch", "seq"), None)
    return jax.shard_map(local, mesh=mesh, in_specs=in_specs, out_specs=out_specs, check_vma=False)
```

```python
import functools
import math

import jax
import jax.numpy as jnp
from jax import lax
from jax.experimental import pallas as pl
from jax.experimental.pallas import tpu as pltpu
from jax.sharding import PartitionSpec as P

MESH = pl.DeviceIdType.MESH
F32 = jnp.float32
BF16 = jnp.bfloat16
N = 8
LANES = 128
TOK = 5
CHUNKS = 24
USED = TOK * CHUNKS
ROWS = 128
PER = 48
MOD = 144
EVERYONE = sorted(
    ((dy, dz) for dy in range(-3, 5) for dz in range(-3, 5) if dy or dz), key=lambda d: (-abs(d[0]) - abs(d[1]), d)
)
OFFSETS = (0, 1, -1, 2, -2, 3, -3, 4)


def by_rows(left, right):
    return lax.dot_general(
        left, right, (((1,), (1,)), ((), ())), preferred_element_type=F32
    )


def kernel(
    states_hbm, step_hbm, plan_hbm, time_hbm, mod_hbm, up_hbm, down_hbm,
    out_ref,
    states_ref, step_ref, plan_ref, time_ref,
    mod_w, up_w, down_w, scaled_w, time_pad, cond_stage, cond_y, cond_z, cond_rows,
    mod_stage, mod_all, shift_rows, bias_ref,
    own_f32, own, gathered, unpack, tokens, partial, pack, rs_in, final_in, final_out,
    gate_pack, raw_pack, own_rows, rows_in, gate_out, gate_in,
    w_sem, small_send, small_recv, g_send, g_recv, rs_send, rs_recv, f_send, f_recv, s_send, s_recv, ready,
):
    section = lax.axis_index("section")
    seq = lax.axis_index("seq")
    z, y = seq // N, lax.rem(seq, N)
    odd = lax.rem(y + z, 2)

    def at(yy, zz):
        return zz * N + yy

    def plus(v, k):
        return lax.rem(v + k + N, N)

    ring_y = [at(plus(y, k), z) for k in range(1, N)]
    ring_z = [at(y, plus(z, k)) for k in range(1, N)]
    far_first = (3, 2, 4, 1, 5, 0, 6)

    barrier = pltpu.get_barrier_semaphore()
    for q in ring_y + ring_z:
        pl.semaphore_signal(barrier, inc=1, device_id={"seq": q}, device_id_type=MESH)
    next_section = lax.rem(section + 1, 4)
    prev_section = lax.rem(section + 3, 4)
    for q in (next_section, prev_section):
        pl.semaphore_signal(barrier, inc=1, device_id={"section": q}, device_id_type=MESH)

    loads = []
    sources = (step_hbm, plan_hbm, time_hbm, states_hbm, mod_hbm.at[0], up_hbm.at[0], down_hbm.at[0])
    targets = (step_ref, plan_ref, time_ref, states_ref, mod_w, up_w, down_w)
    for i, (src, dst) in enumerate(zip(sources, targets)):
        copy = pltpu.make_async_copy(src, dst, w_sem.at[i])
        copy.start()
        loads.append(copy)

    loads[0].wait()
    loads[1].wait()
    index = step_ref[0]
    sigma = plan_ref[index].astype(F32) / 1000.0
    sigma_next = plan_ref[index + 1].astype(F32) / 1000.0
    lane = lax.broadcasted_iota(jnp.int32, (16, LANES), 1).astype(F32)
    angles = (1000.0 * sigma) * jnp.exp(lane * (-math.log(10000.0)) / LANES)
    feature = jnp.concatenate([jnp.cos(angles), jnp.sin(angles)], axis=1).astype(BF16)
    time_pad[...] = jnp.zeros_like(time_pad)
    loads[2].wait()
    time_pad[pl.ds(pl.multiple_of(y * PER, 16), PER), :] = time_ref[...]
    cond = by_rows(feature, time_pad[...])
    cond = (cond * jax.nn.sigmoid(cond)).astype(BF16).astype(F32)
    cond_stage[...] = jnp.zeros_like(cond_stage)
    for m in range(3):
        cond_stage[0, m : m + 1, :] = cond[0:1, m * LANES : (m + 1) * LANES]
    cond_y[y] = cond_stage[0]

    loads[3].wait()
    rows = states_ref[0].astype(F32)
    center = rows - jnp.mean(rows, axis=-1, keepdims=True)
    spread = jnp.mean(center * center, axis=-1, keepdims=True)
    normed = center * lax.rsqrt(spread + 1e-06)
    own_f32[USED:ROWS, :] = jnp.zeros((ROWS - USED, LANES), F32)
    raw_pack[USED:ROWS, :] = jnp.zeros((ROWS - USED, LANES), F32)
    gate_pack[USED:ROWS, :] = jnp.zeros((ROWS - USED, LANES), F32)
    for c in range(CHUNKS):
        own_f32[TOK * c : TOK * c + TOK, :] = normed[:, c * LANES : (c + 1) * LANES]
        raw_pack[TOK * c : TOK * c + TOK, :] = rows[:, c * LANES : (c + 1) * LANES]
    own[...] = own_f32[...].astype(BF16)
    own_rows[...] = raw_pack[...].astype(BF16)
    for i in range(8):
        pack[i, USED:ROWS, :] = jnp.zeros((ROWS - USED, LANES), F32)

    pl.semaphore_wait(barrier, 16)
    pl.semaphore_signal(ready, inc=1, device_id={"section": prev_section}, device_id_type=MESH)

    def send(src, dst, ssem, rsem, q):
        pltpu.make_async_remote_copy(
            src_ref=src, dst_ref=dst, send_sem=ssem, recv_sem=rsem,
            device_id={"seq": q}, device_id_type=MESH,
        ).start()

    def wait(ref, sem):
        pltpu.make_async_copy(ref, ref, sem).wait()

    def pass_on(src, dst, ssem, rsem, q):
        return pltpu.make_async_remote_copy(
            src_ref=src, dst_ref=dst, send_sem=ssem, recv_sem=rsem,
            device_id={"section": next_section, "seq": q}, device_id_type=MESH,
        )

    for k in far_first:
        send(cond_stage.at[0], cond_y.at[y], small_send.at[0], small_recv.at[0], ring_y[k])

    local = pltpu.make_async_copy(own, gathered.at[seq], g_recv.at[seq])
    local.start()
    for k in far_first:
        send(own, gathered.at[seq], g_send.at[0], g_recv.at[seq], ring_y[k] + odd * (ring_z[k] - ring_y[k]))

    rows_copy = pass_on(own_rows, rows_in, s_send.at[0], s_recv.at[0], seq)
    rows_copy.start()

    wait(cond_y.at[0:7], small_recv.at[0])
    total = cond_y[0]
    for i in range(1, N):
        total = total + cond_y[i]
    cond_stage[1] = total
    cond_z[z] = total
    for k in far_first:
        send(cond_stage.at[1], cond_z.at[z], small_send.at[1], small_recv.at[1], ring_z[k])

    up_z, down_z = at(y, plus(z, 1)), at(y, plus(z, -1))
    up_y, down_y = at(plus(y, 1), z), at(plus(y, -1), z)

    def source(odd_class, offset, j):
        if odd_class:
            yy = plus(y, offset)
            return at(yy, 2 * j + lax.rem(yy + 1, 2))
        zz = plus(z, offset)
        return at(2 * j + lax.rem(zz, 2), zz)

    def forward(src, q):
        send(gathered.at[src], gathered.at[src], g_send.at[0], g_recv.at[src], q)

    def slab(offset, odd_class):
        return OFFSETS.index(offset) * 2 + odd_class

    def unpack_slab(offset, odd_class):
        s = slab(offset, odd_class)
        for j in range(4):
            unpack[j] = gathered[source(odd_class, offset, j)].astype(F32)
        for pair in range(2):
            for c in range(CHUNKS):
                both = jnp.concatenate(
                    [
                        unpack[2 * pair, TOK * c : TOK * c + 8, :],
                        unpack[2 * pair + 1, TOK * c : TOK * c + 8, :],
                    ],
                    axis=0,
                )
                tokens[s, 16 * pair : 16 * pair + 16, c * LANES : (c + 1) * LANES] = both.astype(BF16)

    def arrive(offset, odd_class, j):
        src = source(odd_class, offset, j)
        wait(gathered.at[src], g_recv.at[src])
        return src

    for j in range(4):
        for odd_class in (0, 1):
            src = arrive(0, odd_class, j)
            up, down = (up_y, down_y) if odd_class else (up_z, down_z)
            forward(src, up)
            forward(src, down)

    unpack_slab(0, 0)
    unpack_slab(0, 1)

    wait(cond_z.at[0:7], small_recv.at[1])
    for zz in range(N):
        for m in range(3):
            q = zz * 3 + m
            cond_rows[:, q * LANES : (q + 1) * LANES] = jnp.broadcast_to(
                cond_z[zz, m : m + 1, :], (16, LANES)
            ).astype(BF16)
    loads[4].wait()
    modul = by_rows(cond_rows[...], mod_w[...])[0:8]
    wide = jnp.concatenate([modul, jnp.zeros((8, 2 * LANES - MOD), F32)], axis=1)
    placed = wide
    for yy in range(1, N):
        placed = jnp.where(y == yy, pltpu.roll(wide, yy * (MOD - LANES), 1), placed)
    for m in range(2):
        mod_stage[0, m : m + 1, :] = placed[0:1, m * LANES : (m + 1) * LANES]
    mod_all[seq] = mod_stage[0]
    for dy, dz in EVERYONE:
        send(mod_stage.at[0], mod_all.at[seq], small_send.at[2], small_recv.at[2], at(plus(y, dy), plus(z, dz)))

    def gather_step(h):
        for j in range(4):
            for odd_class in (0, 1):
                up, down = (up_y, down_y) if odd_class else (up_z, down_z)
                src = arrive(-h, odd_class, j)
                if h < 3 or j < 2:
                    forward(src, up)
                src = arrive(h, odd_class, j)
                if h < 3 or j >= 2:
                    forward(src, down)

    def unpack_step(h):
        for odd_class in (0, 1):
            unpack_slab(h, odd_class)
            unpack_slab(-h, odd_class)

    gather_step(1)
    unpack_step(1)
    gather_step(2)

    unpack_step(2)
    gather_step(3)
    unpack_step(3)
    for j in range(4):
        for odd_class in (0, 1):
            arrive(4, odd_class, j)
    unpack_slab(4, 0)
    unpack_slab(4, 1)

    wait(mod_all.at[0:63], small_recv.at[2])

    def modulation(q):
        block, m = q // 9 * N, q % 9
        value = jnp.zeros((1, LANES), F32)
        if m < N:
            value = value + mod_all[block + m, 0:1, :]
        if m:
            value = value + mod_all[block + m - 1, 1:2, :]
        return value

    loads[5].wait()
    first = lax.broadcasted_iota(jnp.int32, (16, LANES), 0)
    for c in range(CHUNKS):
        lanes = slice(c * LANES, (c + 1) * LANES)
        scale = 1.0 + modulation(CHUNKS + c)
        scaled_w[:, lanes] = (up_w[:, lanes].astype(F32) * scale).astype(BF16)
        shift = modulation(c)
        high = shift.astype(BF16).astype(F32)
        low = shift - high
        shift_rows[:, lanes] = jnp.where(first == 0, high, jnp.where(first == 1, low, 0.0)).astype(BF16)
    both = by_rows(shift_rows[...], up_w[...])
    bias_ref[...] = jnp.broadcast_to(both[0:1] + both[1:2], bias_ref.shape)
    loads[6].wait()

    for c in range(CHUNKS):
        gate_out[c : c + 1, :] = modulation(2 * CHUNKS + c)
    gate_copy = pass_on(gate_out, gate_in, s_send.at[1], s_recv.at[1], seq)
    gate_copy.start()

    def compute(first_slab, count):
        m = count * 32
        left = tokens[first_slab : first_slab + count].reshape(m, CHUNKS * LANES)
        hidden = jax.nn.gelu(by_rows(left, scaled_w[...]) + bias_ref[0:1, :], approximate=True).astype(BF16)
        for half in range(0, count * 4, 8):
            part = hidden[half * 8 : half * 8 + 64]
            for c4 in range(0, CHUNKS, 4):
                term = jnp.dot(
                    part, down_w[:, c4 * LANES : (c4 + 4) * LANES], preferred_element_type=F32
                )
                for i in range(8):
                    for c in range(4):
                        r = TOK * (c4 + c)
                        pack[i, r : r + TOK, :] = term[8 * i : 8 * i + TOK, c * LANES : (c + 1) * LANES]
            for i in range(8):
                b = half + i
                partial[first_slab + b // 4, b % 4] = pack[i].astype(BF16)

    towards = (up_z, down_z, up_y, down_y)

    def rs_send_to(direction, step, j):
        k = 5 - step
        offset = k if direction % 2 == 0 or k == 4 else -k
        send(
            partial.at[slab(offset, direction // 2), j], rs_in.at[direction, step - 1, j],
            rs_send.at[0], rs_recv.at[direction, step - 1, j], towards[direction],
        )

    def rs_add(direction, step, j):
        k = 5 - step
        offset = k if direction % 2 == 0 else -k
        ref = rs_in.at[direction, step - 2, j]
        wait(ref, rs_recv.at[direction, step - 2, j])
        s = slab(offset, direction // 2)
        partial[s, j] = (partial[s, j].astype(F32) + ref[...].astype(F32)).astype(BF16)

    def halves(direction):
        return (0, 1) if direction % 2 == 0 else (2, 3)

    compute(14, 2)
    for i in range(2):
        for direction in range(4):
            rs_send_to(direction, 1, halves(direction)[i])
    compute(10, 4)
    for i in range(2):
        for direction in range(4):
            rs_send_to(direction, 2, halves(direction + 1)[i])
    for i in range(2):
        for direction in range(4):
            j = halves(direction)[i]
            rs_add(direction, 2, j)
            rs_send_to(direction, 2, j)
    compute(6, 4)
    for step in (3, 4):
        for j in (2, 3, 0, 1):
            for direction in range(4):
                jj = j if direction % 2 == 0 else 3 - j
                rs_add(direction, step, jj)
                rs_send_to(direction, step, jj)
        if step == 3:
            compute(2, 4)
    compute(0, 2)

    wait(gate_in, s_recv.at[1])
    for c in range(CHUNKS):
        gate_pack[TOK * c : TOK * c + TOK, :] = jnp.broadcast_to(gate_in[c : c + 1, :], (TOK, LANES))
    pl.semaphore_wait(ready, 1)

    for j in (2, 3, 0, 1):
        for odd_class in (0, 1):
            value = partial[slab(0, odd_class), j].astype(F32)
            for direction in (2 * odd_class, 2 * odd_class + 1):
                ref = rs_in.at[direction, 3, j]
                wait(ref, rs_recv.at[direction, 3, j])
                value = value + ref[...].astype(F32)
            final_out[odd_class, j] = value.astype(BF16)
            pass_on(
                final_out.at[odd_class, j], final_in.at[z if odd_class else y], f_send.at[0], f_recv.at[0],
                source(odd_class, 0, j),
            ).start()

    wait(final_in, f_recv.at[0])
    branch = final_in[0].astype(F32)
    for i in range(1, N):
        branch = branch + final_in[i].astype(F32)
    wait(rows_in, s_recv.at[0])
    received = (rows_in[...].astype(F32) + gate_pack[...] * branch).astype(BF16).astype(F32)
    moved = raw_pack[...] + (sigma_next - sigma) * received
    own_f32[...] = jnp.where(section == 0, moved, received)
    for c in range(CHUNKS):
        out_ref[0, :, c * LANES : (c + 1) * LANES] = own_f32[TOK * c : TOK * c + TOK, :].astype(BF16)

    for i, ref in enumerate((cond_y.at[0:7], cond_z.at[0:7], mod_all.at[0:63])):
        wait(ref, small_send.at[i])
    wait(gathered.at[0:63], g_send.at[0])
    wait(partial.at[0:14], rs_send.at[0])
    wait(final_in, f_send.at[0])
    rows_copy.wait_send()
    gate_copy.wait_send()


def local(states, step_index, plan, time_weight, mod_weight, up_weight, down_weight):
    vmem = pl.BlockSpec(memory_space=pltpu.VMEM)
    anywhere = pl.BlockSpec(memory_space=pl.ANY)
    dma = pltpu.SemaphoreType.DMA
    width = states.shape[2]
    hidden = up_weight.shape[1]
    block = (ROWS, LANES)
    return pl.pallas_call(
        kernel,
        out_shape=jax.ShapeDtypeStruct(states.shape, states.dtype),
        in_specs=[anywhere] * 7,
        out_specs=vmem,
        scratch_shapes=[
            pltpu.VMEM(states.shape, BF16),
            pltpu.SMEM(step_index.shape, jnp.int32),
            pltpu.SMEM(plan.shape, jnp.int32),
            pltpu.VMEM(time_weight.shape, BF16),
            pltpu.VMEM((MOD, width), BF16),
            pltpu.VMEM((hidden, width), BF16),
            pltpu.VMEM((hidden, width), BF16),
            pltpu.VMEM((hidden, width), BF16),
            pltpu.VMEM((N * PER, 256), BF16),
            pltpu.VMEM((2, 8, LANES), F32),
            pltpu.VMEM((N, 8, LANES), F32),
            pltpu.VMEM((N, 8, LANES), F32),
            pltpu.VMEM((16, width), BF16),
            pltpu.VMEM((1, 2, LANES), F32),
            pltpu.VMEM((64, 2, LANES), F32),
            pltpu.VMEM((16, width), BF16),
            pltpu.VMEM((8, hidden), F32),
            pltpu.VMEM(block, F32),
            pltpu.VMEM(block, BF16),
            pltpu.VMEM((64,) + block, BF16),
            pltpu.VMEM((4,) + block, F32),
            pltpu.VMEM((16, 32, width), BF16),
            pltpu.VMEM((16, 4) + block, BF16),
            pltpu.VMEM((8,) + block, F32),
            pltpu.VMEM((4, 4, 4) + block, BF16),
            pltpu.VMEM((N,) + block, BF16),
            pltpu.VMEM((2, 4) + block, BF16),
            pltpu.VMEM(block, F32),
            pltpu.VMEM(block, F32),
            pltpu.VMEM(block, BF16),
            pltpu.VMEM(block, BF16),
            pltpu.VMEM((CHUNKS, LANES), F32),
            pltpu.VMEM((CHUNKS, LANES), F32),
            dma((7,)), dma((3,)), dma((3,)), dma((1,)), dma((64,)),
            dma((1,)), dma((4, 4, 4)), dma((1,)), dma((1,)), dma((2,)), dma((2,)),
            pltpu.SemaphoreType.REGULAR,
        ],
        name="denoise",
        cost_estimate=pl.CostEstimate(flops=800_000_000, bytes_accessed=3_300_000, transcendentals=100_000),
        compiler_params=pltpu.CompilerParams(
            collective_id=0, has_side_effects=True, vmem_limit_bytes=60 * 1024 * 1024
        ),
    )(states, step_index, plan, time_weight, mod_weight, up_weight, down_weight)


def solution(mesh):
    in_specs = (
        P("section", ("batch", "seq"), None),
        P(),
        P(),
        P("seq", None),
        P("section", "seq", None),
        P("section", "seq", None),
        P("section", "seq", None),
    )
    out_specs = P("section", ("batch", "seq"), None)
    return jax.shard_map(local, mesh=mesh, in_specs=in_specs, out_specs=out_specs, check_vma=False)
```

```python
import functools
import math

import jax
import jax.numpy as jnp
from jax import lax
from jax.experimental import pallas as pl
from jax.experimental.pallas import tpu as pltpu
from jax.sharding import PartitionSpec as P

MESH = pl.DeviceIdType.MESH
F32 = jnp.float32
BF16 = jnp.bfloat16
N = 8
LANES = 128
TOK = 5
CHUNKS = 24
USED = TOK * CHUNKS
ROWS = 120
PER = 48
MOD = 144
EVERYONE = sorted(
    ((dy, dz) for dy in range(-3, 5) for dz in range(-3, 5) if dy or dz), key=lambda d: (-abs(d[0]) - abs(d[1]), d)
)
OFFSETS = (0, 1, -1, 2, -2, 3, -3, 4)


def by_rows(left, right):
    return lax.dot_general(
        left, right, (((1,), (1,)), ((), ())), preferred_element_type=F32
    )


def kernel(
    states_hbm, step_hbm, plan_hbm, time_hbm, mod_hbm, up_hbm, down_hbm,
    out_ref,
    states_ref, step_ref, plan_ref, time_ref,
    mod_w, up_w, down_w, scaled_w, time_pad, cond_stage, cond_y, cond_z, cond_rows,
    mod_stage, mod_all, shift_rows, bias_ref,
    own_f32, own, gathered, unpack, tokens, partial, pack, rs_in, final_in, final_out,
    gate_pack, raw_pack, own_rows, rows_in, gate_out, gate_in,
    w_sem, small_send, small_recv, g_send, g_recv, rs_send, rs_recv, f_send, f_recv, s_send, s_recv, ready,
):
    section = lax.axis_index("section")
    seq = lax.axis_index("seq")
    z, y = seq // N, lax.rem(seq, N)
    odd = lax.rem(y + z, 2)

    def at(yy, zz):
        return zz * N + yy

    def plus(v, k):
        return lax.rem(v + k + N, N)

    ring_y = [at(plus(y, k), z) for k in range(1, N)]
    ring_z = [at(y, plus(z, k)) for k in range(1, N)]
    far_first = (3, 2, 4, 1, 5, 0, 6)

    barrier = pltpu.get_barrier_semaphore()
    for q in ring_y + ring_z:
        pl.semaphore_signal(barrier, inc=1, device_id={"seq": q}, device_id_type=MESH)
    next_section = lax.rem(section + 1, 4)
    prev_section = lax.rem(section + 3, 4)
    for q in (next_section, prev_section):
        pl.semaphore_signal(barrier, inc=1, device_id={"section": q}, device_id_type=MESH)

    loads = []
    sources = (step_hbm, plan_hbm, time_hbm, states_hbm, mod_hbm.at[0], up_hbm.at[0], down_hbm.at[0])
    targets = (step_ref, plan_ref, time_ref, states_ref, mod_w, up_w, down_w)
    for i, (src, dst) in enumerate(zip(sources, targets)):
        copy = pltpu.make_async_copy(src, dst, w_sem.at[i])
        copy.start()
        loads.append(copy)

    loads[0].wait()
    loads[1].wait()
    index = step_ref[0]
    sigma = plan_ref[index].astype(F32) / 1000.0
    sigma_next = plan_ref[index + 1].astype(F32) / 1000.0
    lane = lax.broadcasted_iota(jnp.int32, (16, LANES), 1).astype(F32)
    angles = (1000.0 * sigma) * jnp.exp(lane * (-math.log(10000.0)) / LANES)
    feature = jnp.concatenate([jnp.cos(angles), jnp.sin(angles)], axis=1).astype(BF16)
    time_pad[...] = jnp.zeros_like(time_pad)
    loads[2].wait()
    time_pad[pl.ds(pl.multiple_of(y * PER, 16), PER), :] = time_ref[...]
    cond = by_rows(feature, time_pad[...])
    cond = (cond * jax.nn.sigmoid(cond)).astype(BF16).astype(F32)
    cond_stage[...] = jnp.zeros_like(cond_stage)
    for m in range(3):
        cond_stage[0, m : m + 1, :] = cond[0:1, m * LANES : (m + 1) * LANES]
    cond_y[y] = cond_stage[0]

    loads[3].wait()
    rows = states_ref[0].astype(F32)
    center = rows - jnp.mean(rows, axis=-1, keepdims=True)
    spread = jnp.mean(center * center, axis=-1, keepdims=True)
    normed = center * lax.rsqrt(spread + 1e-06)
    for c in range(CHUNKS):
        own_f32[TOK * c : TOK * c + TOK, :] = normed[:, c * LANES : (c + 1) * LANES]
        raw_pack[TOK * c : TOK * c + TOK, :] = rows[:, c * LANES : (c + 1) * LANES]
    own[...] = own_f32[...].astype(BF16)
    own_rows[...] = raw_pack[...].astype(BF16)
    for i in range(4):
        unpack[i, ROWS:, :] = jnp.zeros((8, LANES), F32)

    pl.semaphore_wait(barrier, 16)
    pl.semaphore_signal(ready, inc=1, device_id={"section": prev_section}, device_id_type=MESH)

    def send(src, dst, ssem, rsem, q):
        pltpu.make_async_remote_copy(
            src_ref=src, dst_ref=dst, send_sem=ssem, recv_sem=rsem,
            device_id={"seq": q}, device_id_type=MESH,
        ).start()

    def wait(ref, sem):
        pltpu.make_async_copy(ref, ref, sem).wait()

    def pass_on(src, dst, ssem, rsem, q):
        return pltpu.make_async_remote_copy(
            src_ref=src, dst_ref=dst, send_sem=ssem, recv_sem=rsem,
            device_id={"section": next_section, "seq": q}, device_id_type=MESH,
        )

    for k in far_first:
        send(cond_stage.at[0], cond_y.at[y], small_send.at[0], small_recv.at[0], ring_y[k])

    local = pltpu.make_async_copy(own, gathered.at[seq], g_recv.at[seq])
    local.start()
    for k in far_first:
        send(own, gathered.at[seq], g_send.at[0], g_recv.at[seq], ring_y[k] + odd * (ring_z[k] - ring_y[k]))

    rows_copy = pass_on(own_rows, rows_in, s_send.at[0], s_recv.at[0], seq)
    rows_copy.start()

    up_z, down_z = at(y, plus(z, 1)), at(y, plus(z, -1))
    up_y, down_y = at(plus(y, 1), z), at(plus(y, -1), z)

    def source(odd_class, offset, j):
        if odd_class:
            yy = plus(y, offset)
            return at(yy, 2 * j + lax.rem(yy + 1, 2))
        zz = plus(z, offset)
        return at(2 * j + lax.rem(zz, 2), zz)

    def forward(src, q):
        send(gathered.at[src], gathered.at[src], g_send.at[0], g_recv.at[src], q)

    def slab(offset, odd_class):
        return OFFSETS.index(offset) * 2 + odd_class

    def unpack_slab(offset, odd_class):
        s = slab(offset, odd_class)
        for j in range(4):
            unpack[j, 0:ROWS, :] = gathered[source(odd_class, offset, j)].astype(F32)
        for pair in range(2):
            for c in range(CHUNKS):
                both = jnp.concatenate(
                    [
                        unpack[2 * pair, TOK * c : TOK * c + 8, :],
                        unpack[2 * pair + 1, TOK * c : TOK * c + 8, :],
                    ],
                    axis=0,
                )
                tokens[s, 16 * pair : 16 * pair + 16, c * LANES : (c + 1) * LANES] = both.astype(BF16)

    def arrive(offset, odd_class, j):
        src = source(odd_class, offset, j)
        wait(gathered.at[src], g_recv.at[src])
        return src

    for j in range(4):
        for odd_class in (0, 1):
            src = arrive(0, odd_class, j)
            up, down = (up_y, down_y) if odd_class else (up_z, down_z)
            forward(src, up)
            forward(src, down)

    wait(cond_y.at[0:7], small_recv.at[0])
    total = cond_y[0]
    for i in range(1, N):
        total = total + cond_y[i]
    cond_stage[1] = total
    cond_z[z] = total
    for k in far_first:
        send(cond_stage.at[1], cond_z.at[z], small_send.at[1], small_recv.at[1], ring_z[k])

    def gather_step(h):
        for j in range(4):
            for odd_class in (0, 1):
                up, down = (up_y, down_y) if odd_class else (up_z, down_z)
                src = arrive(-h, odd_class, j)
                if h < 3 or j < 2:
                    forward(src, up)
                src = arrive(h, odd_class, j)
                if h < 3 or j >= 2:
                    forward(src, down)

    def unpack_step(h):
        for odd_class in (0, 1):
            unpack_slab(h, odd_class)
            unpack_slab(-h, odd_class)

    gather_step(1)
    wait(cond_z.at[0:7], small_recv.at[1])
    for zz in range(N):
        for m in range(3):
            q = zz * 3 + m
            cond_rows[:, q * LANES : (q + 1) * LANES] = jnp.broadcast_to(
                cond_z[zz, m : m + 1, :], (16, LANES)
            ).astype(BF16)
    loads[4].wait()
    modul = by_rows(cond_rows[...], mod_w[...])[0:8]
    wide = jnp.concatenate([modul, jnp.zeros((8, 2 * LANES - MOD), F32)], axis=1)
    placed = wide
    for yy in range(1, N):
        placed = jnp.where(y == yy, pltpu.roll(wide, yy * (MOD - LANES), 1), placed)
    for m in range(2):
        mod_stage[0, m : m + 1, :] = placed[0:1, m * LANES : (m + 1) * LANES]
    mod_all[seq] = mod_stage[0]
    for dy, dz in EVERYONE:
        send(mod_stage.at[0], mod_all.at[seq], small_send.at[2], small_recv.at[2], at(plus(y, dy), plus(z, dz)))

    unpack_slab(0, 0)
    unpack_slab(0, 1)
    gather_step(2)

    unpack_step(1)
    gather_step(3)
    unpack_step(2)
    unpack_step(3)

    wait(mod_all.at[0:63], small_recv.at[2])

    def modulation(q):
        block, m = q // 9 * N, q % 9
        value = jnp.zeros((1, LANES), F32)
        if m < N:
            value = value + mod_all[block + m, 0:1, :]
        if m:
            value = value + mod_all[block + m - 1, 1:2, :]
        return value

    loads[5].wait()
    first = lax.broadcasted_iota(jnp.int32, (16, LANES), 0)
    for c in range(CHUNKS):
        lanes = slice(c * LANES, (c + 1) * LANES)
        scale = 1.0 + modulation(CHUNKS + c)
        scaled_w[:, lanes] = (up_w[:, lanes].astype(F32) * scale).astype(BF16)
        shift = modulation(c)
        high = shift.astype(BF16).astype(F32)
        low = shift - high
        shift_rows[:, lanes] = jnp.where(first == 0, high, jnp.where(first == 1, low, 0.0)).astype(BF16)
    both = by_rows(shift_rows[...], up_w[...])
    bias_ref[...] = jnp.broadcast_to(both[0:1] + both[1:2], bias_ref.shape)
    loads[6].wait()

    for c in range(CHUNKS):
        gate_out[c : c + 1, :] = modulation(2 * CHUNKS + c)
    gate_copy = pass_on(gate_out, gate_in, s_send.at[1], s_recv.at[1], seq)
    gate_copy.start()

    for j in range(4):
        for odd_class in (0, 1):
            arrive(4, odd_class, j)
    unpack_slab(4, 0)
    unpack_slab(4, 1)

    def compute(first_slab, count):
        m = count * 32
        left = tokens[first_slab : first_slab + count].reshape(m, CHUNKS * LANES)
        hidden = jax.nn.gelu(by_rows(left, scaled_w[...]) + bias_ref[0:1, :], approximate=True).astype(BF16)
        for half in range(0, count * 4, 8):
            part = hidden[half * 8 : half * 8 + 64]
            for c4 in range(0, CHUNKS, 4):
                term = jnp.dot(
                    part, down_w[:, c4 * LANES : (c4 + 4) * LANES], preferred_element_type=F32
                )
                for i in range(8):
                    for c in range(4):
                        r = TOK * (c4 + c)
                        pack[i, r : r + TOK, :] = term[8 * i : 8 * i + TOK, c * LANES : (c + 1) * LANES]
            for i in range(8):
                b = half + i
                partial[first_slab + b // 4, b % 4] = pack[i].astype(BF16)

    towards = (up_z, down_z, up_y, down_y)

    def rs_send_to(direction, step, j):
        k = 5 - step
        offset = k if direction % 2 == 0 or k == 4 else -k
        send(
            partial.at[slab(offset, direction // 2), j], rs_in.at[direction, step - 1, j],
            rs_send.at[0], rs_recv.at[direction, step - 1, j], towards[direction],
        )

    def rs_add(direction, step, j):
        k = 5 - step
        offset = k if direction % 2 == 0 else -k
        ref = rs_in.at[direction, step - 2, j]
        wait(ref, rs_recv.at[direction, step - 2, j])
        s = slab(offset, direction // 2)
        partial[s, j] = (partial[s, j].astype(F32) + ref[...].astype(F32)).astype(BF16)

    def halves(direction):
        return (0, 1) if direction % 2 == 0 else (2, 3)

    compute(14, 2)
    for i in range(2):
        for direction in range(4):
            rs_send_to(direction, 1, halves(direction)[i])
    compute(10, 4)
    for i in range(2):
        for direction in range(4):
            rs_send_to(direction, 2, halves(direction + 1)[i])
    for i in range(2):
        for direction in range(4):
            j = halves(direction)[i]
            rs_add(direction, 2, j)
            rs_send_to(direction, 2, j)
    compute(6, 4)
    for step in (3, 4):
        for j in (2, 3, 0, 1):
            for direction in range(4):
                jj = j if direction % 2 == 0 else 3 - j
                rs_add(direction, step, jj)
                rs_send_to(direction, step, jj)
        if step == 3:
            compute(2, 4)
    compute(0, 2)

    wait(gate_in, s_recv.at[1])
    for c in range(CHUNKS):
        gate_pack[TOK * c : TOK * c + TOK, :] = jnp.broadcast_to(gate_in[c : c + 1, :], (TOK, LANES))
    pl.semaphore_wait(ready, 1)

    for j in (2, 3, 0, 1):
        for odd_class in (0, 1):
            value = partial[slab(0, odd_class), j].astype(F32)
            for direction in (2 * odd_class, 2 * odd_class + 1):
                ref = rs_in.at[direction, 3, j]
                wait(ref, rs_recv.at[direction, 3, j])
                value = value + ref[...].astype(F32)
            final_out[odd_class, j] = value.astype(BF16)
            pass_on(
                final_out.at[odd_class, j], final_in.at[z if odd_class else y], f_send.at[0], f_recv.at[0],
                source(odd_class, 0, j),
            ).start()

    wait(final_in, f_recv.at[0])
    branch = final_in[0].astype(F32)
    for i in range(1, N):
        branch = branch + final_in[i].astype(F32)
    wait(rows_in, s_recv.at[0])
    received = (rows_in[...].astype(F32) + gate_pack[...] * branch).astype(BF16).astype(F32)
    moved = raw_pack[...] + (sigma_next - sigma) * received
    own_f32[...] = jnp.where(section == 0, moved, received)
    for c in range(CHUNKS):
        out_ref[0, :, c * LANES : (c + 1) * LANES] = own_f32[TOK * c : TOK * c + TOK, :].astype(BF16)

    for i, ref in enumerate((cond_y.at[0:7], cond_z.at[0:7], mod_all.at[0:63])):
        wait(ref, small_send.at[i])
    wait(gathered.at[0:63], g_send.at[0])
    wait(partial.at[0:14], rs_send.at[0])
    wait(final_in, f_send.at[0])
    rows_copy.wait_send()
    gate_copy.wait_send()


def local(states, step_index, plan, time_weight, mod_weight, up_weight, down_weight):
    vmem = pl.BlockSpec(memory_space=pltpu.VMEM)
    anywhere = pl.BlockSpec(memory_space=pl.ANY)
    dma = pltpu.SemaphoreType.DMA
    width = states.shape[2]
    hidden = up_weight.shape[1]
    block = (ROWS, LANES)
    return pl.pallas_call(
        kernel,
        out_shape=jax.ShapeDtypeStruct(states.shape, states.dtype),
        in_specs=[anywhere] * 7,
        out_specs=vmem,
        scratch_shapes=[
            pltpu.VMEM(states.shape, BF16),
            pltpu.SMEM(step_index.shape, jnp.int32),
            pltpu.SMEM(plan.shape, jnp.int32),
            pltpu.VMEM(time_weight.shape, BF16),
            pltpu.VMEM((MOD, width), BF16),
            pltpu.VMEM((hidden, width), BF16),
            pltpu.VMEM((hidden, width), BF16),
            pltpu.VMEM((hidden, width), BF16),
            pltpu.VMEM((N * PER, 256), BF16),
            pltpu.VMEM((2, 8, LANES), F32),
            pltpu.VMEM((N, 8, LANES), F32),
            pltpu.VMEM((N, 8, LANES), F32),
            pltpu.VMEM((16, width), BF16),
            pltpu.VMEM((1, 2, LANES), F32),
            pltpu.VMEM((64, 2, LANES), F32),
            pltpu.VMEM((16, width), BF16),
            pltpu.VMEM((8, hidden), F32),
            pltpu.VMEM(block, F32),
            pltpu.VMEM(block, BF16),
            pltpu.VMEM((64,) + block, BF16),
            pltpu.VMEM((4, ROWS + 8, LANES), F32),
            pltpu.VMEM((16, 32, width), BF16),
            pltpu.VMEM((16, 4) + block, BF16),
            pltpu.VMEM((8,) + block, F32),
            pltpu.VMEM((4, 4, 4) + block, BF16),
            pltpu.VMEM((N,) + block, BF16),
            pltpu.VMEM((2, 4) + block, BF16),
            pltpu.VMEM(block, F32),
            pltpu.VMEM(block, F32),
            pltpu.VMEM(block, BF16),
            pltpu.VMEM(block, BF16),
            pltpu.VMEM((CHUNKS, LANES), F32),
            pltpu.VMEM((CHUNKS, LANES), F32),
            dma((7,)), dma((3,)), dma((3,)), dma((1,)), dma((64,)),
            dma((1,)), dma((4, 4, 4)), dma((1,)), dma((1,)), dma((2,)), dma((2,)),
            pltpu.SemaphoreType.REGULAR,
        ],
        name="denoise",
        cost_estimate=pl.CostEstimate(flops=800_000_000, bytes_accessed=3_300_000, transcendentals=100_000),
        compiler_params=pltpu.CompilerParams(
            collective_id=0, has_side_effects=True, vmem_limit_bytes=60 * 1024 * 1024
        ),
    )(states, step_index, plan, time_weight, mod_weight, up_weight, down_weight)


def solution(mesh):
    in_specs = (
        P("section", ("batch", "seq"), None),
        P(),
        P(),
        P("seq", None),
        P("section", "seq", None),
        P("section", "seq", None),
        P("section", "seq", None),
    )
    out_specs = P("section", ("batch", "seq"), None)
    return jax.shard_map(local, mesh=mesh, in_specs=in_specs, out_specs=out_specs, check_vma=False)
```

```python
import functools
import math

import jax
import jax.numpy as jnp
from jax import lax
from jax.experimental import pallas as pl
from jax.experimental.pallas import tpu as pltpu
from jax.sharding import PartitionSpec as P

MESH = pl.DeviceIdType.MESH
F32 = jnp.float32
BF16 = jnp.bfloat16
N = 8
LANES = 128
TOK = 5
CHUNKS = 24
USED = TOK * CHUNKS
ROWS = 120
PER = 48
MOD = 144
EVERYONE = sorted(
    ((dy, dz) for dy in range(-3, 5) for dz in range(-3, 5) if dy or dz), key=lambda d: (-abs(d[0]) - abs(d[1]), d)
)
OFFSETS = (0, 1, -1, 2, -2, 3, -3, 4)


def by_rows(left, right):
    return lax.dot_general(
        left, right, (((1,), (1,)), ((), ())), preferred_element_type=F32
    )


def kernel(
    states_hbm, step_hbm, plan_hbm, time_hbm, mod_hbm, up_hbm, down_hbm,
    out_ref,
    states_ref, step_ref, plan_ref, time_ref,
    mod_w, up_w, down_w, scaled_w, time_pad, cond_stage, cond_y, cond_z, cond_rows,
    mod_stage, mod_all, shift_rows, bias_ref,
    own_f32, own, gathered, unpack, tokens, partial, pack, rs_in, final_in, final_out,
    gate_pack, raw_pack, own_rows, rows_in, gate_out, gate_in,
    w_sem, small_send, small_recv, g_send, g_recv, rs_send, rs_recv, f_send, f_recv, s_send, s_recv, ready,
):
    section = lax.axis_index("section")
    seq = lax.axis_index("seq")
    z, y = seq // N, lax.rem(seq, N)
    odd = lax.rem(y + z, 2)

    def at(yy, zz):
        return zz * N + yy

    def plus(v, k):
        return lax.rem(v + k + N, N)

    ring_y = [at(plus(y, k), z) for k in range(1, N)]
    ring_z = [at(y, plus(z, k)) for k in range(1, N)]
    far_first = (3, 2, 4, 1, 5, 0, 6)

    barrier = pltpu.get_barrier_semaphore()
    for q in ring_y + ring_z:
        pl.semaphore_signal(barrier, inc=1, device_id={"seq": q}, device_id_type=MESH)
    next_section = lax.rem(section + 1, 4)
    prev_section = lax.rem(section + 3, 4)
    for q in (next_section, prev_section):
        pl.semaphore_signal(barrier, inc=1, device_id={"section": q}, device_id_type=MESH)

    loads = []
    sources = (step_hbm, plan_hbm, time_hbm, states_hbm, mod_hbm.at[0], up_hbm.at[0], down_hbm.at[0])
    targets = (step_ref, plan_ref, time_ref, states_ref, mod_w, up_w, down_w)
    for i, (src, dst) in enumerate(zip(sources, targets)):
        copy = pltpu.make_async_copy(src, dst, w_sem.at[i])
        copy.start()
        loads.append(copy)

    loads[0].wait()
    loads[1].wait()
    index = step_ref[0]
    sigma = plan_ref[index].astype(F32) / 1000.0
    sigma_next = plan_ref[index + 1].astype(F32) / 1000.0
    lane = lax.broadcasted_iota(jnp.int32, (16, LANES), 1).astype(F32)
    angles = (1000.0 * sigma) * jnp.exp(lane * (-math.log(10000.0)) / LANES)
    feature = jnp.concatenate([jnp.cos(angles), jnp.sin(angles)], axis=1).astype(BF16)
    time_pad[...] = jnp.zeros_like(time_pad)
    loads[2].wait()
    time_pad[pl.ds(pl.multiple_of(y * PER, 16), PER), :] = time_ref[...]
    cond = by_rows(feature, time_pad[...])
    cond = (cond * jax.nn.sigmoid(cond)).astype(BF16).astype(F32)
    cond_stage[...] = jnp.zeros_like(cond_stage)
    for m in range(3):
        cond_stage[0, m : m + 1, :] = cond[0:1, m * LANES : (m + 1) * LANES]
    cond_y[y] = cond_stage[0]

    loads[3].wait()
    rows = states_ref[0].astype(F32)
    center = rows - jnp.mean(rows, axis=-1, keepdims=True)
    spread = jnp.mean(center * center, axis=-1, keepdims=True)
    normed = center * lax.rsqrt(spread + 1e-06)
    for c in range(CHUNKS):
        own_f32[TOK * c : TOK * c + TOK, :] = normed[:, c * LANES : (c + 1) * LANES]
        raw_pack[TOK * c : TOK * c + TOK, :] = rows[:, c * LANES : (c + 1) * LANES]
    own[...] = own_f32[...].astype(BF16)
    own_rows[...] = raw_pack[...].astype(BF16)
    for i in range(4):
        unpack[i, ROWS:, :] = jnp.zeros((8, LANES), F32)

    pl.semaphore_wait(barrier, 16)
    pl.semaphore_signal(ready, inc=1, device_id={"section": prev_section}, device_id_type=MESH)

    def send(src, dst, ssem, rsem, q):
        pltpu.make_async_remote_copy(
            src_ref=src, dst_ref=dst, send_sem=ssem, recv_sem=rsem,
            device_id={"seq": q}, device_id_type=MESH,
        ).start()

    def wait(ref, sem):
        pltpu.make_async_copy(ref, ref, sem).wait()

    def pass_on(src, dst, ssem, rsem, q):
        return pltpu.make_async_remote_copy(
            src_ref=src, dst_ref=dst, send_sem=ssem, recv_sem=rsem,
            device_id={"section": next_section, "seq": q}, device_id_type=MESH,
        )

    for k in far_first:
        send(cond_stage.at[0], cond_y.at[y], small_send.at[0], small_recv.at[0], ring_y[k])

    local = pltpu.make_async_copy(own, gathered.at[seq], g_recv.at[seq])
    local.start()
    for k in far_first:
        send(own, gathered.at[seq], g_send.at[0], g_recv.at[seq], ring_y[k] + odd * (ring_z[k] - ring_y[k]))


    up_z, down_z = at(y, plus(z, 1)), at(y, plus(z, -1))
    up_y, down_y = at(plus(y, 1), z), at(plus(y, -1), z)

    def source(odd_class, offset, j):
        if odd_class:
            yy = plus(y, offset)
            return at(yy, 2 * j + lax.rem(yy + 1, 2))
        zz = plus(z, offset)
        return at(2 * j + lax.rem(zz, 2), zz)

    def forward(src, q):
        send(gathered.at[src], gathered.at[src], g_send.at[0], g_recv.at[src], q)

    def slab(offset, odd_class):
        return OFFSETS.index(offset) * 2 + odd_class

    def unpack_slab(offset, odd_class):
        s = slab(offset, odd_class)
        for j in range(4):
            unpack[j, 0:ROWS, :] = gathered[source(odd_class, offset, j)].astype(F32)
        for pair in range(2):
            for c in range(CHUNKS):
                both = jnp.concatenate(
                    [
                        unpack[2 * pair, TOK * c : TOK * c + 8, :],
                        unpack[2 * pair + 1, TOK * c : TOK * c + 8, :],
                    ],
                    axis=0,
                )
                tokens[s, 16 * pair : 16 * pair + 16, c * LANES : (c + 1) * LANES] = both.astype(BF16)

    def arrive(offset, odd_class, j):
        src = source(odd_class, offset, j)
        wait(gathered.at[src], g_recv.at[src])
        return src

    for j in range(4):
        for odd_class in (0, 1):
            src = arrive(0, odd_class, j)
            up, down = (up_y, down_y) if odd_class else (up_z, down_z)
            forward(src, up)
            forward(src, down)

    wait(cond_y.at[0:7], small_recv.at[0])
    total = cond_y[0]
    for i in range(1, N):
        total = total + cond_y[i]
    cond_stage[1] = total
    cond_z[z] = total
    for k in far_first:
        send(cond_stage.at[1], cond_z.at[z], small_send.at[1], small_recv.at[1], ring_z[k])

    def gather_step(h):
        for j in range(4):
            for odd_class in (0, 1):
                up, down = (up_y, down_y) if odd_class else (up_z, down_z)
                src = arrive(-h, odd_class, j)
                if h < 3 or j < 2:
                    forward(src, up)
                src = arrive(h, odd_class, 3 - j)
                if h < 3 or j < 2:
                    forward(src, down)

    def unpack_step(h):
        for odd_class in (0, 1):
            unpack_slab(h, odd_class)
            unpack_slab(-h, odd_class)

    gather_step(1)
    wait(cond_z.at[0:7], small_recv.at[1])
    for zz in range(N):
        for m in range(3):
            q = zz * 3 + m
            cond_rows[:, q * LANES : (q + 1) * LANES] = jnp.broadcast_to(
                cond_z[zz, m : m + 1, :], (16, LANES)
            ).astype(BF16)
    loads[4].wait()
    modul = by_rows(cond_rows[...], mod_w[...])[0:8]
    wide = jnp.concatenate([modul, jnp.zeros((8, 2 * LANES - MOD), F32)], axis=1)
    placed = wide
    for yy in range(1, N):
        placed = jnp.where(y == yy, pltpu.roll(wide, yy * (MOD - LANES), 1), placed)
    for m in range(2):
        mod_stage[0, m : m + 1, :] = placed[0:1, m * LANES : (m + 1) * LANES]
    mod_all[seq] = mod_stage[0]
    for dy, dz in EVERYONE:
        send(mod_stage.at[0], mod_all.at[seq], small_send.at[2], small_recv.at[2], at(plus(y, dy), plus(z, dz)))

    unpack_slab(0, 0)
    unpack_slab(0, 1)
    gather_step(2)

    unpack_step(1)
    gather_step(3)
    rows_copy = pass_on(own_rows, rows_in, s_send.at[0], s_recv.at[0], seq)
    rows_copy.start()
    unpack_step(2)
    unpack_step(3)

    wait(mod_all.at[0:63], small_recv.at[2])

    def modulation(q):
        block, m = q // 9 * N, q % 9
        value = jnp.zeros((1, LANES), F32)
        if m < N:
            value = value + mod_all[block + m, 0:1, :]
        if m:
            value = value + mod_all[block + m - 1, 1:2, :]
        return value

    loads[5].wait()
    first = lax.broadcasted_iota(jnp.int32, (16, LANES), 0)
    for c in range(CHUNKS):
        lanes = slice(c * LANES, (c + 1) * LANES)
        scale = 1.0 + modulation(CHUNKS + c)
        scaled_w[:, lanes] = (up_w[:, lanes].astype(F32) * scale).astype(BF16)
        shift = modulation(c)
        high = shift.astype(BF16).astype(F32)
        low = shift - high
        shift_rows[:, lanes] = jnp.where(first == 0, high, jnp.where(first == 1, low, 0.0)).astype(BF16)
    both = by_rows(shift_rows[...], up_w[...])
    bias_ref[...] = jnp.broadcast_to(both[0:1] + both[1:2], bias_ref.shape)
    loads[6].wait()

    for c in range(CHUNKS):
        gate_out[c : c + 1, :] = modulation(2 * CHUNKS + c)
    gate_copy = pass_on(gate_out, gate_in, s_send.at[1], s_recv.at[1], seq)
    gate_copy.start()

    for j in range(4):
        for odd_class in (0, 1):
            arrive(4, odd_class, j)
    unpack_slab(4, 0)
    unpack_slab(4, 1)

    def compute(first_slab, count):
        m = count * 32
        left = tokens[first_slab : first_slab + count].reshape(m, CHUNKS * LANES)
        hidden = jax.nn.gelu(by_rows(left, scaled_w[...]) + bias_ref[0:1, :], approximate=True).astype(BF16)
        for half in range(0, count * 4, 8):
            part = hidden[half * 8 : half * 8 + 64]
            for c4 in range(0, CHUNKS, 4):
                term = jnp.dot(
                    part, down_w[:, c4 * LANES : (c4 + 4) * LANES], preferred_element_type=F32
                )
                for i in range(8):
                    for c in range(4):
                        r = TOK * (c4 + c)
                        pack[i, r : r + TOK, :] = term[8 * i : 8 * i + TOK, c * LANES : (c + 1) * LANES]
            for i in range(8):
                b = half + i
                partial[first_slab + b // 4, b % 4] = pack[i].astype(BF16)

    towards = (up_z, down_z, up_y, down_y)

    def rs_send_to(direction, step, j):
        k = 5 - step
        offset = k if direction % 2 == 0 or k == 4 else -k
        send(
            partial.at[slab(offset, direction // 2), j], rs_in.at[direction, step - 1, j],
            rs_send.at[0], rs_recv.at[direction, step - 1, j], towards[direction],
        )

    def rs_add(direction, step, j):
        k = 5 - step
        offset = k if direction % 2 == 0 else -k
        ref = rs_in.at[direction, step - 2, j]
        wait(ref, rs_recv.at[direction, step - 2, j])
        s = slab(offset, direction // 2)
        partial[s, j] = (partial[s, j].astype(F32) + ref[...].astype(F32)).astype(BF16)

    def halves(direction):
        return (0, 1) if direction % 2 == 0 else (2, 3)

    compute(14, 2)
    for i in range(2):
        for direction in range(4):
            rs_send_to(direction, 1, halves(direction)[i])
    compute(10, 4)
    for i in range(2):
        for direction in range(4):
            rs_send_to(direction, 2, halves(direction + 1)[i])
    for i in range(2):
        for direction in range(4):
            j = halves(direction)[i]
            rs_add(direction, 2, j)
            rs_send_to(direction, 2, j)
    compute(6, 4)
    for step in (3, 4):
        for j in (2, 3, 0, 1):
            for direction in range(4):
                jj = j if direction % 2 == 0 else 3 - j
                rs_add(direction, step, jj)
                rs_send_to(direction, step, jj)
        if step == 3:
            compute(2, 4)
    compute(0, 2)

    wait(gate_in, s_recv.at[1])
    for c in range(CHUNKS):
        gate_pack[TOK * c : TOK * c + TOK, :] = jnp.broadcast_to(gate_in[c : c + 1, :], (TOK, LANES))
    pl.semaphore_wait(ready, 1)

    for j in (2, 3, 0, 1):
        for odd_class in (0, 1):
            value = partial[slab(0, odd_class), j].astype(F32)
            for direction in (2 * odd_class, 2 * odd_class + 1):
                ref = rs_in.at[direction, 3, j]
                wait(ref, rs_recv.at[direction, 3, j])
                value = value + ref[...].astype(F32)
            final_out[odd_class, j] = value.astype(BF16)
            pass_on(
                final_out.at[odd_class, j], final_in.at[z if odd_class else y], f_send.at[0], f_recv.at[0],
                source(odd_class, 0, j),
            ).start()

    wait(final_in, f_recv.at[0])
    branch = final_in[0].astype(F32)
    for i in range(1, N):
        branch = branch + final_in[i].astype(F32)
    wait(rows_in, s_recv.at[0])
    received = (rows_in[...].astype(F32) + gate_pack[...] * branch).astype(BF16).astype(F32)
    moved = raw_pack[...] + (sigma_next - sigma) * received
    own_f32[...] = jnp.where(section == 0, moved, received)
    for c in range(CHUNKS):
        out_ref[0, :, c * LANES : (c + 1) * LANES] = own_f32[TOK * c : TOK * c + TOK, :].astype(BF16)

    for i, ref in enumerate((cond_y.at[0:7], cond_z.at[0:7], mod_all.at[0:63])):
        wait(ref, small_send.at[i])
    wait(gathered.at[0:63], g_send.at[0])
    wait(partial.at[0:14], rs_send.at[0])
    wait(final_in, f_send.at[0])
    rows_copy.wait_send()
    gate_copy.wait_send()


def local(states, step_index, plan, time_weight, mod_weight, up_weight, down_weight):
    vmem = pl.BlockSpec(memory_space=pltpu.VMEM)
    anywhere = pl.BlockSpec(memory_space=pl.ANY)
    dma = pltpu.SemaphoreType.DMA
    width = states.shape[2]
    hidden = up_weight.shape[1]
    block = (ROWS, LANES)
    return pl.pallas_call(
        kernel,
        out_shape=jax.ShapeDtypeStruct(states.shape, states.dtype),
        in_specs=[anywhere] * 7,
        out_specs=vmem,
        scratch_shapes=[
            pltpu.VMEM(states.shape, BF16),
            pltpu.SMEM(step_index.shape, jnp.int32),
            pltpu.SMEM(plan.shape, jnp.int32),
            pltpu.VMEM(time_weight.shape, BF16),
            pltpu.VMEM((MOD, width), BF16),
            pltpu.VMEM((hidden, width), BF16),
            pltpu.VMEM((hidden, width), BF16),
            pltpu.VMEM((hidden, width), BF16),
            pltpu.VMEM((N * PER, 256), BF16),
            pltpu.VMEM((2, 8, LANES), F32),
            pltpu.VMEM((N, 8, LANES), F32),
            pltpu.VMEM((N, 8, LANES), F32),
            pltpu.VMEM((16, width), BF16),
            pltpu.VMEM((1, 2, LANES), F32),
            pltpu.VMEM((64, 2, LANES), F32),
            pltpu.VMEM((16, width), BF16),
            pltpu.VMEM((8, hidden), F32),
            pltpu.VMEM(block, F32),
            pltpu.VMEM(block, BF16),
            pltpu.VMEM((64,) + block, BF16),
            pltpu.VMEM((4, ROWS + 8, LANES), F32),
            pltpu.VMEM((16, 32, width), BF16),
            pltpu.VMEM((16, 4) + block, BF16),
            pltpu.VMEM((8,) + block, F32),
            pltpu.VMEM((4, 4, 4) + block, BF16),
            pltpu.VMEM((N,) + block, BF16),
            pltpu.VMEM((2, 4) + block, BF16),
            pltpu.VMEM(block, F32),
            pltpu.VMEM(block, F32),
            pltpu.VMEM(block, BF16),
            pltpu.VMEM(block, BF16),
            pltpu.VMEM((CHUNKS, LANES), F32),
            pltpu.VMEM((CHUNKS, LANES), F32),
            dma((7,)), dma((3,)), dma((3,)), dma((1,)), dma((64,)),
            dma((1,)), dma((4, 4, 4)), dma((1,)), dma((1,)), dma((2,)), dma((2,)),
            pltpu.SemaphoreType.REGULAR,
        ],
        name="denoise",
        cost_estimate=pl.CostEstimate(flops=800_000_000, bytes_accessed=3_300_000, transcendentals=100_000),
        compiler_params=pltpu.CompilerParams(
            collective_id=0, has_side_effects=True, vmem_limit_bytes=60 * 1024 * 1024
        ),
    )(states, step_index, plan, time_weight, mod_weight, up_weight, down_weight)


def solution(mesh):
    in_specs = (
        P("section", ("batch", "seq"), None),
        P(),
        P(),
        P("seq", None),
        P("section", "seq", None),
        P("section", "seq", None),
        P("section", "seq", None),
    )
    out_specs = P("section", ("batch", "seq"), None)
    return jax.shard_map(local, mesh=mesh, in_specs=in_specs, out_specs=out_specs, check_vma=False)
```
